32 devices in a mesh: row: 4 (over y, x), col: 4 (over z), depth: 2 (over core).
Axes of the slice: x: 2, y: 2, z: 4, core: 2. Of those that a mesh axis runs over, the one named last changes fastest.
Arguments:
- matrix: float32 [6144, 6144], P('row', ('col', 'depth')), as said below
- occupancy: int32 [48, 48], replicated, may hold values from 0 to 1, as said below
- pattern: int32 [48, 48], replicated, may hold values 0 or 1
Outputs:
- square: float32 [6144, 6144], P('row', ('col', 'depth'))
The draws below stay inside these ranges and needn't reach their ends.
Inputs may be any that keep to these rules, and one draw needn't show every extreme that they name: matrix is symmetric. occupancy is symmetric, every diagonal block is occupied, and every block row holds exactly 4 occupied blocks.
All inputs are finite; a program needn't handle non-finite values.
Results may differ from the reference program's by a relative error of at most 0.000055.
Values sent between devices are 32-bit elements; how exact they have to be, the bound alone decides.
No kernel may reach another device: no remote copies, remote signals or barrier semaphores. Data moves between devices by JAX's collectives and lax.ppermute only.
A program may use at most 192 MiB of HBM per device.

```python
import jax
import jax.numpy as jnp
from jax import lax

BS = 128
KB = 4
NB = 48
N = 6144


def draw_matrix(key, part):
    key = jax.random.fold_in(key, 11)
    scale = 2.5 * (KB * BS) ** (-0.5)
    base = jax.random.normal(key, (N, N), jnp.float32)
    return (base + base.T) * (0.5 * scale)


def draw_occupancy(key, part):
    key = jax.random.fold_in(key, 12)
    places = jax.random.permutation(key, NB).astype(jnp.int32)
    differ = jnp.bitwise_xor(places[:, None], places[None, :])
    linked = (differ == 0).astype(jnp.int32)
    for bit in range(KB - 1):
        linked = jnp.maximum(linked, (differ == 1 << bit).astype(jnp.int32))
    return linked


def place_ends(entries, stream_key, smallest, largest):
    longest = entries.shape.index(max(entries.shape))
    spots = []
    for shift in (0, 1):
        where = [jax.random.randint(jax.random.fold_in(stream_key, axis), (), 0, length) for axis, length in enumerate(entries.shape)]
        where[longest] = (where[longest] + shift) % entries.shape[longest]
        spots.append(tuple(where))
    return entries.at[spots[0]].set(smallest).at[spots[1]].set(largest)


def setup_inputs(seed: int = 0) -> dict:
    key_list = jax.random.split(jax.random.key(seed), 4)
    return {
        "matrix": draw_matrix(jax.random.fold_in(key_list[3], 71), 0),
        "occupancy": draw_occupancy(jax.random.fold_in(key_list[3], 71), 0),
        "pattern": place_ends((jax.random.randint(key_list[2], (NB, NB), 0, 4) < 3).astype(jnp.int32), jax.random.fold_in(key_list[2], 1), 0, 1),
    }


def expand_mask(mask):
    return jnp.repeat(jnp.repeat(mask.astype(jnp.float32), BS, axis=0), BS, axis=1)


def reference(matrix, occupancy, pattern):
    masked = matrix * expand_mask(occupancy)
    full = jnp.dot(masked, masked, precision=lax.Precision.HIGHEST, preferred_element_type=jnp.float32)
    return full * expand_mask(pattern)
```

```python
import functools

import jax
import jax.numpy as jnp
from jax import lax
from jax.experimental import pallas as pl
from jax.experimental.pallas import tpu as pltpu
from jax.sharding import PartitionSpec as P

BS = 128
KB = 4
NONE = 31
GROUP = 4
PAT_BIT = 20
PLAIN, LOWER, UPPER = 0, 1, 2


class Sizes:
    def __init__(self, mesh, matrix_shape):
        self.n_row = mesh.shape["row"]
        self.n_col = mesh.shape["col"]
        self.n_depth = mesh.shape["depth"]
        self.nb = matrix_shape[0] // BS
        self.rows = self.nb // self.n_row
        self.cols = self.nb // (self.n_col * self.n_depth)
        self.pairs = (min(self.rows, self.cols) + 1) // 2
        self.own = KB * self.cols
        self.n_a = KB * self.rows
        self.n_out = self.rows * self.cols
        self.cap = KB * min(self.rows, self.cols)
        self.x_tables = -(-self.n_row // GROUP)
        self.z_tables = -(-self.n_col // GROUP)
        self.tables = self.x_tables + self.z_tables
        self.buckets = []
        for far, near in ((5, 12), (6, 12), (7, 12), (8, 14), (9, 14), (11, 16)):
            if near < self.cap:
                self.buckets.append((far, near))
        self.buckets.append((self.cap, self.cap))


def group_of(place, size, count):
    group = jnp.zeros_like(place)
    for g in range(1, count):
        group = group + (place >= g * size).astype(jnp.int32)
    return group


def ones_dot(a, b):
    return jnp.dot(a.astype(jnp.bfloat16), b.astype(jnp.bfloat16), preferred_element_type=jnp.float32)


def table_kernel(sz, occ_ref, pat_ref, table_ref, near_ref, bucket_ref):
    nb = sz.nb
    occ = (occ_ref[...] != 0).astype(jnp.float32)
    pat = (pat_ref[...] != 0).astype(jnp.float32)
    row_i = lax.broadcasted_iota(jnp.int32, (nb, nb), 0)
    col_i = lax.broadcasted_iota(jnp.int32, (nb, nb), 1)
    off = jnp.where(row_i == col_i, 0.0, occ)
    row_rg = group_of(row_i, sz.rows, sz.n_row)
    col_rg = group_of(col_i, sz.rows, sz.n_row)
    row_cg = group_of(row_i, sz.cols, sz.n_col * sz.n_depth)
    col_cg = group_of(col_i, sz.cols, sz.n_col * sz.n_depth)
    col_zg = group_of(col_i, sz.cols * sz.n_depth, sz.n_col)
    same = row_cg == col_cg
    before = (same & (row_i < col_i)).astype(jnp.float32)
    same = same.astype(jnp.float32)
    above = ((row_rg == col_rg) & (col_i < row_i)).astype(jnp.float32)
    first = jnp.maximum(row_rg * sz.rows, col_cg * sz.cols)
    last = jnp.minimum((row_rg + 1) * sz.rows, (col_cg + 1) * sz.cols)
    skip = jnp.where(first < last, sz.pairs, 0)

    def codes(need, sent):
        listed = jnp.where(need > 0, off, 0.0)
        rank = ones_dot(listed, before) + ones_dot(above, ones_dot(listed, same))
        rank = rank.astype(jnp.int32) + skip
        used = jnp.where(listed > 0, rank + 1, skip)
        return jnp.where(listed > 0, jnp.minimum(rank, NONE - 1), NONE), jnp.where(sent, used, 0), jnp.where(sent, 0, used)

    far = jnp.zeros((nb, nb), jnp.int32)
    near = jnp.zeros((nb, nb), jnp.int32)
    tables = [jnp.zeros((nb, nb), jnp.int32) for _ in range(sz.tables)]
    for r in range(sz.n_row):
        need = ones_dot(jnp.where(col_rg == r, occ, 0.0), pat)
        code, count, _ = codes(need, row_rg != r)
        far = jnp.maximum(far, count)
        tables[r // GROUP] += code << (5 * (r % GROUP))
    for z in range(sz.n_col):
        need = ones_dot(jnp.where(col_zg == z, pat, 0.0), occ)
        code, count, here = codes(need, col_zg != z)
        far = jnp.maximum(far, count)
        near = jnp.maximum(near, here)
        tables[sz.x_tables + z // GROUP] += code << (5 * (z % GROUP))
    tables[0] += pat.astype(jnp.int32) << PAT_BIT
    for t in range(sz.tables):
        table_ref[t] = tables[t]

    lower = (col_i < row_i).astype(jnp.float32)
    order = ones_dot(lower, occ).astype(jnp.int32)
    weight = jnp.where(occ > 0, row_i << (6 * jnp.minimum(order, KB - 1)), 0)
    near_ref[...] = jnp.sum(weight, axis=0, keepdims=True)
    far_max = jnp.max(far)
    near_max = jnp.max(near)
    bucket = jnp.int32(0)
    for c, s in sz.buckets[:-1]:
        bucket = bucket + jnp.where((far_max <= c) & (near_max <= s), 0, 1)
    bucket_ref[0] = bucket


def neighbour(near_ref, block, s):
    return (near_ref[0, block] >> (6 * s)) & 63


def slot_of(near_ref, block, other):
    slot = jnp.int32(0)
    for u in range(KB):
        slot = slot + (neighbour(near_ref, block, u) < other).astype(jnp.int32)
    return slot


def code_at(table_ref, i, k, group, base):
    word = table_ref[base + group // GROUP, i, k]
    return (word >> (5 * (group % GROUP))) & 31


def place(ref, slot):
    return ref.at[pl.ds(pl.multiple_of(slot * BS, BS), BS), :]


def block_at(ref, i, j):
    return ref.at[pl.ds(pl.multiple_of(i * BS, BS), BS), pl.ds(pl.multiple_of(j * BS, BS), BS)]


def pack_kernel(sz, table_ref, near_ref, matrix_ref, own_ref, *rest):
    n_x = sz.n_row - 1
    outs, sem = rest[:-1], rest[-1]
    row = lax.axis_index("row")
    z = lax.axis_index("col")
    c = z * sz.n_depth + lax.axis_index("depth")

    def at(e):
        j, s = e // KB, e % KB
        k = c * sz.cols + j
        i = neighbour(near_ref, k, s)
        local = i - row * sz.rows
        return i, k, local, j, (local >= 0) & (local < sz.rows)

    def fetch(e, started):
        _, _, local, j, mine = at(e)

        @pl.when(mine)
        def _():
            pltpu.make_async_copy(block_at(matrix_ref, local, j), place(own_ref, e), sem).start()

        return started + mine.astype(jnp.int32)

    started = lax.fori_loop(0, sz.own, fetch, jnp.int32(0))

    def landed(_, carry):
        pltpu.make_async_copy(block_at(matrix_ref, 0, 0), place(own_ref, 0), sem).wait()
        return carry

    lax.fori_loop(0, started, landed, 0)

    first = jnp.maximum(row * sz.rows, c * sz.cols)
    last = jnp.minimum((row + 1) * sz.rows, (c + 1) * sz.cols)

    @pl.when(first < last)
    def _():
        down = lax.broadcasted_iota(jnp.int32, (BS, BS), 0)
        across = lax.broadcasted_iota(jnp.int32, (BS, BS), 1)
        count = min(sz.rows, sz.cols)
        for p in range(sz.pairs):
            d = first + 2 * p
            low = place(own_ref, (d - c * sz.cols) * KB + slot_of(near_ref, d, d))[...]
            if 2 * p + 1 < count:
                d = d + 1
                high = place(own_ref, (d - c * sz.cols) * KB + slot_of(near_ref, d, d))[...]
            else:
                high = jnp.zeros_like(low)
            both = jnp.where(down >= across, low, high)
            line = jnp.sum(jnp.where(down == across, high, 0.0), axis=0, keepdims=True)
            for out in outs:
                out[p * BS : (p + 1) * BS, :] = both
                out[out.shape[0] - 8 + p : out.shape[0] - 7 + p, :] = line

    def visit(e, carry):
        i, k, _, _, mine = at(e)

        @pl.when(mine & (i != k))
        def _():
            block = place(own_ref, e)[...]
            codes = []
            for m in range(1, sz.n_row):
                codes.append(code_at(table_ref, i, k, row ^ m, 0))
            for m in range(sz.n_col):
                codes.append(code_at(table_ref, i, k, z ^ m, sz.x_tables))
            for out, code in zip(outs, codes, strict=True):
                @pl.when(code != NONE)
                def _(out=out, code=code):
                    place(out, code)[...] = block

        return carry

    lax.fori_loop(0, sz.own, visit, 0)


def plan_kernel(sz, table_ref, near_ref, load_ref, job_ref, count_ref, zeros_ref, used_ref, blank_ref, sem):
    row = lax.axis_index("row")
    z = lax.axis_index("col")
    depth = lax.axis_index("depth")
    c = z * sz.n_depth + depth
    n_x, n_z = sz.n_row - 1, sz.n_col - 1

    blank_ref[...] = jnp.zeros_like(blank_ref)

    def wipe(i):
        return pltpu.make_async_copy(blank_ref, zeros_ref.at[pl.ds(pl.multiple_of(i * BS, BS), BS), :], sem)

    for i in range(sz.rows):
        wipe(i).start()

    def clear(e, carry):
        used_ref[e] = 0
        return carry

    lax.fori_loop(0, sz.n_a + sz.own, clear, 0)

    def find(e, n):
        local, j = e // sz.cols, e % sz.cols
        i, col = row * sz.rows + local, c * sz.cols + j
        kept = ((table_ref[0, i, col] >> PAT_BIT) & 1) == 1

        def search(n):
            start = n
            for s in range(KB):
                k = neighbour(near_ref, col, s)
                for t in range(KB):
                    hit = neighbour(near_ref, i, t) == k

                    @pl.when(hit)
                    def _(n=n, s=s, t=t):
                        job_ref[n, 0] = local * KB + t
                        job_ref[n, 1] = j * KB + s
                        job_ref[n, 2] = e
                        job_ref[n, 3] = (n == start).astype(jnp.int32)
                        used_ref[local * KB + t] = 1
                        used_ref[sz.n_a + j * KB + s] = 1

                    n = n + hit.astype(jnp.int32)

            @pl.when(n > start)
            def _():
                job_ref[n - 1, 3] = job_ref[n - 1, 3] + 2

            return n

        return lax.cond(kept, search, lambda n: n, n)

    count_ref[0] = lax.fori_loop(0, sz.n_out, find, jnp.int32(0))

    def add(n, source, code, dst, i, k, mine, sender_first):
        slot = jnp.where(mine, (k - c * sz.cols) * KB + slot_of(near_ref, k, i), code)
        packed = (i == k) & ~mine
        place_in = i - sender_first
        load_ref[n, 0] = jnp.where(mine, 0, source)
        load_ref[n, 1] = jnp.where(packed, place_in >> 1, slot)
        load_ref[n, 2] = jnp.where(packed, LOWER + (place_in & 1), PLAIN)
        load_ref[n, 3] = dst

    def load_a(e, n):
        local, t = e // KB, e % KB
        i = row * sz.rows + local
        k = neighbour(near_ref, i, t)

        @pl.when(used_ref[e] == 1)
        def _():
            kc = k // sz.cols
            m, q = (kc // sz.n_depth) ^ z, (kc % sz.n_depth) ^ depth
            across = 1 + n_x + n_z + (q - 1) * sz.n_col + m
            source = jnp.where(q == 0, n_x + m, across)
            code = code_at(table_ref, i, k, z, sz.x_tables)
            add(n, source, code, e, i, k, kc == c, jnp.maximum(row * sz.rows, kc * sz.cols))

        return n + used_ref[e]

    n = lax.fori_loop(0, sz.n_a, load_a, jnp.int32(0))

    def load_b(e, n):
        j, s = e // KB, e % KB
        col = c * sz.cols + j
        k = neighbour(near_ref, col, s)

        @pl.when(used_ref[sz.n_a + e] == 1)
        def _():
            kr = k // sz.rows
            code = code_at(table_ref, k, col, row, 0)
            add(n, kr ^ row, code, sz.n_a + e, k, col, kr == row, jnp.maximum(kr * sz.rows, c * sz.cols))

        return n + used_ref[sz.n_a + e]

    count_ref[1] = lax.fori_loop(0, sz.own, load_b, n)
    for i in range(sz.rows):
        wipe(i).wait()


def product_kernel(sz, load_ref, job_ref, count_ref, zeros_ref, *rest):
    del zeros_ref
    n_in = 1 + sz.n_row - 1 + sz.n_col - 1 + (sz.n_depth - 1) * sz.n_col
    sources = rest[:n_in]
    out_ref, high_ref, low_ref, acc_ref, sem = rest[n_in:]
    down = lax.broadcasted_iota(jnp.int32, (BS, BS), 0)
    across = lax.broadcasted_iota(jnp.int32, (BS, BS), 1)

    def load(n, carry):
        source, slot, kind, dst = (load_ref[n, f] for f in range(4))

        def keep(x):
            high = x.astype(jnp.bfloat16)
            place(high_ref, dst)[...] = high
            place(low_ref, dst)[...] = (x - high.astype(jnp.float32)).astype(jnp.bfloat16)

        for s, ref in enumerate(sources):
            @pl.when(source == s)
            def _(s=s, ref=ref):
                x = place(ref, slot)[...]
                if s == 0:
                    keep(x)
                    return

                @pl.when(kind == PLAIN)
                def _():
                    keep(x)

                @pl.when(kind == LOWER)
                def _():
                    keep(jnp.where(down >= across, x, x.T))

                @pl.when(kind == UPPER)
                def _():
                    line = ref[pl.ds(ref.shape[0] - 8 + slot, 1), :]
                    keep(jnp.where(down < across, x, jnp.where(down > across, x.T, line)))

        return carry

    lax.fori_loop(0, count_ref[1], load, 0)

    def multiply(n, stored):
        a, b, target, ends = (job_ref[n, f] for f in range(4))
        ah, al = place(high_ref, a)[...], place(low_ref, a)[...]
        bh, bl = place(high_ref, sz.n_a + b)[...], place(low_ref, sz.n_a + b)[...]
        dot = functools.partial(jnp.dot, preferred_element_type=jnp.float32)
        value = dot(ah, bh) + (dot(ah, bl) + dot(al, bh))
        acc = place(acc_ref, target)
        acc[...] = jnp.where((ends & 1) == 1, 0.0, acc[...]) + value

        @pl.when(ends >= 2)
        def _():
            pltpu.make_async_copy(acc, block_at(out_ref, target // sz.cols, target % sz.cols), sem).start()

        return stored + (ends >> 1)

    stored = lax.fori_loop(0, count_ref[0], multiply, jnp.int32(0))

    def written(_, carry):
        pltpu.make_async_copy(place(acc_ref, 0), block_at(out_ref, 0, 0), sem).wait()
        return carry

    lax.fori_loop(0, stored, written, 0)


def swaps(size, m):
    return [(i, i ^ m) for i in range(size)]


def exchange_and_multiply(sz, far, near, matrix, table, near_list):
    n_x, n_z = sz.n_row - 1, sz.n_col - 1
    smem = pl.BlockSpec(memory_space=pltpu.SMEM)
    vmem = pl.BlockSpec(memory_space=pltpu.VMEM)
    anywhere = pl.BlockSpec(memory_space=pl.ANY)

    def blocks(n):
        return jax.ShapeDtypeStruct((n * BS, BS), jnp.float32)

    far_shape = jax.ShapeDtypeStruct((far * BS + 8, BS), jnp.float32)
    near_shape = jax.ShapeDtypeStruct((near * BS + 8, BS), jnp.float32)
    own, *packed = pl.pallas_call(
        functools.partial(pack_kernel, sz),
        out_shape=[blocks(sz.own)] + [far_shape] * n_x + [near_shape] + [far_shape] * n_z,
        in_specs=[smem, smem, anywhere],
        out_specs=[vmem] * (2 + n_x + n_z),
        scratch_shapes=[pltpu.SemaphoreType.DMA],
        compiler_params=pltpu.CompilerParams(vmem_limit_bytes=32 * 2**20),
        name="pack",
    )(table, near_list, matrix)
    loads, jobs, counts, zeros = pl.pallas_call(
        functools.partial(plan_kernel, sz),
        out_shape=[
            jax.ShapeDtypeStruct((sz.n_a + sz.own, 4), jnp.int32),
            jax.ShapeDtypeStruct((sz.own * KB, 4), jnp.int32),
            jax.ShapeDtypeStruct((2,), jnp.int32),
            jax.ShapeDtypeStruct(matrix.shape, matrix.dtype),
        ],
        in_specs=[smem, smem],
        out_specs=[smem, smem, smem, anywhere],
        scratch_shapes=[
            pltpu.SMEM((sz.n_a + sz.own,), jnp.int32),
            pltpu.VMEM((BS, matrix.shape[1]), jnp.float32),
            pltpu.SemaphoreType.DMA,
        ],
        cost_estimate=pl.CostEstimate(flops=0, bytes_accessed=20_000_000, transcendentals=0),
        name="plan",
    )(table, near_list)
    zs = [lax.ppermute(packed[n_x + m], "col", swaps(sz.n_col, m)) for m in range(n_z, 0, -1)][::-1]
    xs = [lax.ppermute(packed[m - 1], "row", swaps(sz.n_row, m)) for m in range(n_x, 0, -1)][::-1]
    ds = []
    for q in range(1, sz.n_depth):
        for block_list in [packed[n_x]] + zs:
            ds.append(lax.ppermute(block_list, "depth", swaps(sz.n_depth, q)))
    sources = [own, *xs, *zs, *ds]
    return pl.pallas_call(
        functools.partial(product_kernel, sz),
        out_shape=jax.ShapeDtypeStruct(matrix.shape, matrix.dtype),
        in_specs=[smem] * 3 + [anywhere] + [vmem] * len(sources),
        out_specs=anywhere,
        input_output_aliases={3: 0},
        scratch_shapes=[
            pltpu.VMEM(((sz.n_a + sz.own) * BS, BS), jnp.bfloat16),
            pltpu.VMEM(((sz.n_a + sz.own) * BS, BS), jnp.bfloat16),
            pltpu.VMEM((sz.n_out * BS, BS), jnp.float32),
            pltpu.SemaphoreType.DMA,
        ],
        compiler_params=pltpu.CompilerParams(vmem_limit_bytes=40 * 2**20),
        name="product",
    )(loads, jobs, counts, zeros, *sources)


def shards(sz, matrix, occupancy, pattern):
    smem = pl.BlockSpec(memory_space=pltpu.SMEM)
    vmem = pl.BlockSpec(memory_space=pltpu.VMEM)
    table, near_list, bucket = pl.pallas_call(
        functools.partial(table_kernel, sz),
        out_shape=[
            jax.ShapeDtypeStruct((sz.tables, sz.nb, sz.nb), jnp.int32),
            jax.ShapeDtypeStruct((1, sz.nb), jnp.int32),
            jax.ShapeDtypeStruct((1,), jnp.int32),
        ],
        in_specs=[vmem, vmem],
        out_specs=[vmem, vmem, smem],
        name="tables",
    )(occupancy, pattern)
    branches = [functools.partial(exchange_and_multiply, sz, far, near) for far, near in sz.buckets]
    return lax.switch(bucket[0], branches, matrix, table, near_list)


def solution(mesh):
    def whole(matrix, occupancy, pattern):
        sz = Sizes(mesh, matrix.shape)
        return jax.shard_map(
            functools.partial(shards, sz),
            mesh=mesh,
            in_specs=(P("row", ("col", "depth")), P(), P()),
            out_specs=P("row", ("col", "depth")),
            check_vma=False,
        )(matrix, occupancy, pattern)

    return whole
```

```python
import functools

import jax
import jax.numpy as jnp
from jax import lax
from jax.experimental import pallas as pl
from jax.experimental.pallas import tpu as pltpu
from jax.sharding import PartitionSpec as P

BS = 128
KB = 4
NONE = 31
GROUP = 6
PAT_BIT = 30
PLAIN, LOWER, UPPER = 0, 1, 2
UNROLL = 4


class Sizes:
    def __init__(self, mesh, matrix_shape):
        self.n_row = mesh.shape["row"]
        self.n_col = mesh.shape["col"]
        self.n_depth = mesh.shape["depth"]
        self.nb = matrix_shape[0] // BS
        self.rows = self.nb // self.n_row
        self.cols = self.nb // (self.n_col * self.n_depth)
        self.pairs = (min(self.rows, self.cols) + 1) // 2
        self.own = KB * self.cols
        self.n_a = KB * self.rows
        self.n_load = self.n_a + self.own
        self.n_job = self.own * KB
        self.n_out = self.rows * self.cols
        self.cap = KB * min(self.rows, self.cols)
        self.stages = 2
        self.jobs_at = self.stages * self.n_load
        self.targets_at = self.jobs_at + self.stages * (self.n_job + UNROLL)
        self.counts_at = self.targets_at + self.n_out
        self.n_plan = self.counts_at + 2 * self.stages + 1
        self.x_tables = -(-self.n_row // GROUP)
        self.tables = self.x_tables + -(-self.n_col // GROUP)
        self.block = self.n_col
        self.lengths = []
        for far in (5, 6, 7, 8, 9, 10, 12):
            if far + 5 < self.cap:
                self.lengths.append((far, far + 1, far + 2, far + 5))
        self.lengths.append((self.cap,) * 4)


def group_of(place, size, count):
    group = jnp.zeros_like(place)
    for g in range(1, count):
        group = group + (place >= g * size).astype(jnp.int32)
    return group


def ones_dot(a, b):
    return jnp.dot(a.astype(jnp.bfloat16), b.astype(jnp.bfloat16), preferred_element_type=jnp.float32)


def table_kernel(sz, occ_ref, pat_ref, table_ref, near_ref, bucket_ref):
    nb = sz.nb
    occ = (occ_ref[...] != 0).astype(jnp.float32)
    pat = (pat_ref[...] != 0).astype(jnp.float32)
    row_i = lax.broadcasted_iota(jnp.int32, (nb, nb), 0)
    col_i = lax.broadcasted_iota(jnp.int32, (nb, nb), 1)
    off = jnp.where(row_i == col_i, 0.0, occ)
    row_rg = group_of(row_i, sz.rows, sz.n_row)
    col_rg = group_of(col_i, sz.rows, sz.n_row)
    row_cg = group_of(row_i, sz.cols, sz.n_col * sz.n_depth)
    col_cg = group_of(col_i, sz.cols, sz.n_col * sz.n_depth)
    col_zg = group_of(col_i, sz.cols * sz.n_depth, sz.n_col)
    same = row_cg == col_cg
    before = (same & (row_i < col_i)).astype(jnp.float32)
    same = same.astype(jnp.float32)
    above = ((row_rg == col_rg) & (col_i < row_i)).astype(jnp.float32)
    first = jnp.maximum(row_rg * sz.rows, col_cg * sz.cols)
    last = jnp.minimum((row_rg + 1) * sz.rows, (col_cg + 1) * sz.cols)
    skip = jnp.where(first < last, sz.pairs, 0)

    def codes(need, sent):
        listed = jnp.where(need > 0, off, 0.0)
        rank = ones_dot(listed, before) + ones_dot(above, ones_dot(listed, same))
        rank = rank.astype(jnp.int32) + skip
        used = jnp.where(listed > 0, rank + 1, skip)
        return jnp.where(listed > 0, jnp.minimum(rank, NONE - 1), NONE), jnp.where(sent, used, 0), jnp.where(sent, 0, used)

    most = [jnp.zeros((nb, nb), jnp.int32) for _ in range(4)]
    tables = [jnp.zeros((nb, nb), jnp.int32) for _ in range(sz.tables)]
    for r in range(sz.n_row):
        need = ones_dot(jnp.where(col_rg == r, occ, 0.0), pat)
        code, count, _ = codes(need, row_rg != r)
        most[2] = jnp.maximum(most[2], count)
        tables[r // GROUP] += code << (5 * (r % GROUP))
    for z in range(sz.n_col):
        need = ones_dot(jnp.where(col_zg == z, pat, 0.0), occ)
        code, count, here = codes(need, col_zg != z)
        side = col_zg == (z ^ 1)
        most[0] = jnp.maximum(most[0], jnp.where(side, 0, count))
        most[1] = jnp.maximum(most[1], jnp.where(side, count, 0))
        most[3] = jnp.maximum(most[3], here)
        tables[sz.x_tables + z // GROUP] += code << (5 * (z % GROUP))
    tables[0] += pat.astype(jnp.int32) << PAT_BIT
    for t in range(sz.tables):
        table_ref[t] = tables[t]

    lower = (col_i < row_i).astype(jnp.float32)
    order = ones_dot(lower, occ).astype(jnp.int32)
    weight = jnp.where(occ > 0, row_i << (6 * jnp.minimum(order, KB - 1)), 0)
    near_ref[...] = jnp.sum(weight, axis=0, keepdims=True)
    bucket = jnp.zeros((nb, nb), jnp.int32)
    for lengths in sz.lengths[:-1]:
        over = most[0] > lengths[0]
        for count, length in zip(most[1:], lengths[1:], strict=True):
            over = over | (count > length)
        bucket = bucket + over.astype(jnp.int32)
    bucket_ref[0] = jnp.max(bucket)


def neighbour(near_ref, block, s):
    return (near_ref[0, block] >> (6 * s)) & 63


def slot_of(near_ref, block, other):
    slot = jnp.int32(0)
    for u in range(KB):
        slot = slot + (neighbour(near_ref, block, u) < other).astype(jnp.int32)
    return slot


def code_at(table_ref, i, k, group, base):
    word = table_ref[base + group // GROUP, i, k]
    return (word >> (5 * (group % GROUP))) & 31


def place(ref, slot):
    return ref.at[pl.ds(pl.multiple_of(slot * BS, BS), BS), :]


def block_at(ref, i, j):
    return ref.at[pl.ds(pl.multiple_of(i * BS, BS), BS), pl.ds(pl.multiple_of(j * BS, BS), BS)]


def own_slot(sz, near_ref, i, k, c):
    return (k - c * sz.cols) * KB + slot_of(near_ref, k, i)


def repeat(first, last, body):
    def step(n, carry):
        body(n)
        return carry

    lax.fori_loop(first, last, step, 0)


def pack_kernel(sz, table_ref, near_ref, matrix_ref, own_ref, *rest):
    outs, sems = rest[:-1], rest[-1]
    row = lax.axis_index("row")
    z = lax.axis_index("col")
    c = z * sz.n_depth + lax.axis_index("depth")

    def at(e):
        k = c * sz.cols + e // KB
        i = neighbour(near_ref, k, e % KB)
        return i, k, (i >= row * sz.rows) & (i < (row + 1) * sz.rows)

    def fetching(e, i):
        block = block_at(matrix_ref, jnp.clip(i - row * sz.rows, 0, sz.rows - 1), e // KB)
        return pltpu.make_async_copy(block, place(own_ref, e), sems.at[e])

    def fetch(e):
        i, _, mine = at(e)

        @pl.when(mine)
        def _():
            fetching(e, i).start()

    repeat(0, sz.own, fetch)

    codes = [(sz.x_tables, z ^ m) for m in range(sz.n_col)] + [(0, row ^ m) for m in range(1, sz.n_row)]

    def visit(e):
        i, k, mine = at(e)

        @pl.when(mine)
        def _():
            fetching(e, i).wait()

        @pl.when(mine & (i != k))
        def _():
            block = place(own_ref, e)[...]
            for out, (base, group) in zip(outs, codes, strict=True):
                code = code_at(table_ref, i, k, group, base)

                @pl.when(code != NONE)
                def _(out=out, code=code):
                    place(out, code)[...] = block

    repeat(0, sz.own, visit)

    first = jnp.maximum(row * sz.rows, c * sz.cols)
    last = jnp.minimum((row + 1) * sz.rows, (c + 1) * sz.cols)

    @pl.when(first < last)
    def _():
        down = lax.broadcasted_iota(jnp.int32, (BS, BS), 0)
        across = lax.broadcasted_iota(jnp.int32, (BS, BS), 1)
        for p in range(sz.pairs):
            d = first + 2 * p
            low = place(own_ref, own_slot(sz, near_ref, d, d, c))[...]
            if 2 * p + 1 < min(sz.rows, sz.cols):
                high = place(own_ref, own_slot(sz, near_ref, d + 1, d + 1, c))[...]
            else:
                high = jnp.zeros_like(low)
            both = jnp.where(down >= across, low, high)
            line = jnp.sum(jnp.where(down == across, high, 0.0), axis=0, keepdims=True)
            for out in outs:
                out[p * BS : (p + 1) * BS, :] = both
                out[out.shape[0] - 8 + p : out.shape[0] - 7 + p, :] = line


def plan_kernel(sz, table_ref, near_ref, plan_ref, zeros_ref, slot_ref, seen_ref, blank_ref, sem):
    row = lax.axis_index("row")
    z = lax.axis_index("col")
    depth = lax.axis_index("depth")
    c = z * sz.n_depth + depth
    n_x = sz.n_row - 1

    blank_ref[...] = jnp.zeros_like(blank_ref)

    def wipe(i):
        return pltpu.make_async_copy(blank_ref, zeros_ref.at[pl.ds(pl.multiple_of(i * BS, BS), BS), :], sem)

    for i in range(sz.rows):
        wipe(i).start()

    def clear(ref, size):
        def step(e, carry):
            ref[e] = 0
            return carry

        lax.fori_loop(0, size, step, 0)

    clear(slot_ref, sz.n_load)
    clear(seen_ref, sz.n_out)

    def stage_of(k):
        kc = k // sz.cols
        kz = kc // sz.n_depth
        near = (kc % sz.n_depth == depth) & (kz >> 1 == z >> 1)
        return jnp.where(near, 0, 1)

    def count(counts, stage):
        return tuple(n + (stage == q).astype(jnp.int32) for q, n in enumerate(counts))

    def spot(counts, stage, size):
        n = counts[0]
        for q in range(1, sz.stages):
            n = jnp.where(stage == q, counts[q], n)
        return n + stage * size

    def find(e, carry):
        j, s = e // KB, e % KB
        col = c * sz.cols + j
        k = neighbour(near_ref, col, s)
        stage = stage_of(k)
        for t in range(KB):
            i = neighbour(near_ref, k, t)
            local = i - row * sz.rows
            mine = (local >= 0) & (local < sz.rows)
            kept = mine & (((table_ref[0, i, col] >> PAT_BIT) & 1) == 1)

            def add(carry, i=i, local=local):
                counts, targets = carry
                a = local * KB + slot_of(near_ref, i, k)
                target = local * sz.cols + j
                known = seen_ref[target]
                at = sz.jobs_at + spot(counts, stage, sz.n_job + UNROLL)
                plan_ref[at] = a + (e << 8) + (target << 16)
                slot_ref[a] = 1
                slot_ref[sz.n_a + e] = 1
                seen_ref[target] = 1

                @pl.when(known == 0)
                def _():
                    plan_ref[sz.targets_at + targets] = target

                return count(counts, stage), targets + 1 - known

            carry = lax.cond(kept, add, lambda carry: carry, carry)
        return carry

    none = (jnp.int32(0),) * sz.stages
    jobs, n_targets = lax.fori_loop(0, sz.own, find, (none, jnp.int32(0)))
    for q in range(sz.stages):
        for u in range(UNROLL):
            plan_ref[sz.jobs_at + q * (sz.n_job + UNROLL) + jobs[q] + u] = sz.n_out << 16

    def add(n, source, code, dst, i, k, mine, sender_first):
        slot = jnp.where(mine, own_slot(sz, near_ref, i, k, c), code)
        packed = (i == k) & ~mine
        order = i - sender_first
        source = jnp.where(mine, 0, source)
        slot = jnp.where(packed, order >> 1, slot)
        kind = jnp.where(packed, LOWER + (order & 1), PLAIN)
        plan_ref[n] = source + (slot << 8) + (kind << 16) + (dst << 18)

    def load_b(e, counts):
        j, s = e // KB, e % KB
        col = c * sz.cols + j

        def take(counts):
            k = neighbour(near_ref, col, s)
            kr = k // sz.rows
            code = code_at(table_ref, k, col, row, 0)
            sender = jnp.maximum(kr * sz.rows, c * sz.cols)
            add(counts[0], kr ^ row, code, sz.n_a + e, k, col, kr == row, sender)
            return count(counts, jnp.int32(0))

        return lax.cond(slot_ref[sz.n_a + e] == 1, take, lambda counts: counts, counts)

    def load_a(e, counts):
        local, t = e // KB, e % KB
        i = row * sz.rows + local

        def take(counts):
            k = neighbour(near_ref, i, t)
            kc = k // sz.cols
            kz, kd = kc // sz.n_depth, kc % sz.n_depth
            q = kd ^ depth
            stage = stage_of(k)
            code = code_at(table_ref, i, k, z, sz.x_tables)
            source = 1 + n_x + q * sz.block + (kz ^ z) - 1
            add(spot(counts, stage, sz.n_load), source, code, e, i, k, kc == c, jnp.maximum(row * sz.rows, kc * sz.cols))
            return count(counts, stage)

        return lax.cond(slot_ref[e] == 1, take, lambda counts: counts, counts)

    loads = lax.fori_loop(0, sz.own, load_b, none)
    loads = lax.fori_loop(0, sz.n_a, load_a, loads)
    for q in range(sz.stages):
        plan_ref[sz.counts_at + 2 * q] = loads[q]
        plan_ref[sz.counts_at + 2 * q + 1] = (jobs[q] + UNROLL - 1) // UNROLL
    plan_ref[sz.counts_at + 2 * sz.stages] = n_targets
    for i in range(sz.rows):
        wipe(i).wait()


def load_block(word, sources, a_ref, b_ref, n_a):
    source, slot, kind, dst = word & 255, (word >> 8) & 255, (word >> 16) & 3, word >> 18

    def keep(x):
        high = x.astype(jnp.bfloat16)
        low = (x - high.astype(jnp.float32)).astype(jnp.bfloat16)
        if b_ref is None:
            a_out = place(a_ref, dst)
            a_out[:, :BS], a_out[:, BS : 2 * BS], a_out[:, 2 * BS :] = high, low, high
            return

        @pl.when(dst < n_a)
        def _():
            a_out = place(a_ref, dst)
            a_out[:, :BS], a_out[:, BS : 2 * BS], a_out[:, 2 * BS :] = high, low, high

        @pl.when(dst >= n_a)
        def _():
            for p, part in enumerate((high, high, low)):
                place(b_ref, 3 * (dst - n_a) + p)[...] = part

    for s, ref in sources:
        @pl.when(source == s)
        def _(s=s, ref=ref):
            x = place(ref, slot)[...]
            if s == 0:
                keep(x)
                return

            @pl.when(kind == PLAIN)
            def _():
                keep(x)

            @pl.when(kind != PLAIN)
            def _():
                down = lax.broadcasted_iota(jnp.int32, (BS, BS), 0)
                across = lax.broadcasted_iota(jnp.int32, (BS, BS), 1)
                lower = kind == LOWER
                line = ref[pl.ds(ref.shape[0] - 8 + slot, 1), :]
                stored = (down > across) == lower
                edge = jnp.where(lower, x, line)
                keep(jnp.where(down == across, edge, jnp.where(stored, x, x.T)))


def run_stage(sz, stage, plan_ref, sources, a_ref, b_new_ref, b_ref, acc_ref):
    first = stage * sz.n_load
    repeat(
        first,
        first + plan_ref[sz.counts_at + 2 * stage],
        lambda n: load_block(plan_ref[n], sources, a_ref, b_new_ref, sz.n_a),
    )
    jobs = sz.jobs_at + stage * (sz.n_job + UNROLL)

    def multiply(n):
        words = [plan_ref[jobs + UNROLL * n + u] for u in range(UNROLL)]
        values = []
        for word in words:
            left = place(a_ref, word & 255)[...]
            b = pl.multiple_of(((word >> 8) & 255) * (3 * BS), 3 * BS)
            right = b_ref[pl.ds(b, 3 * BS), :]
            values.append(jnp.dot(left, right, preferred_element_type=jnp.float32))
        for word, value in zip(words, values, strict=True):
            place(acc_ref, word >> 16)[...] += value

    repeat(0, plan_ref[sz.counts_at + 2 * stage + 1], multiply)


def early_kernel(sz, numbers, plan_ref, *rest):
    sources = list(zip(numbers, rest[:-3], strict=True))
    b_ref, acc_ref, a_ref = rest[-3:]
    acc_ref[...] = jnp.zeros_like(acc_ref)
    run_stage(sz, 0, plan_ref, sources, a_ref, b_ref, b_ref, acc_ref)


def carry_on(sz, plan_ref, before_ref, acc_ref):
    def copy(n):
        target = plan_ref[sz.targets_at + n]
        place(acc_ref, target)[...] = place(before_ref, target)[...]

    repeat(0, plan_ref[sz.counts_at + 2 * sz.stages], copy)


def late_kernel(sz, numbers, plan_ref, zeros_ref, b_ref, before_ref, *rest):
    del zeros_ref
    sources = list(zip(numbers, rest[:-4], strict=True))
    out_ref, a_ref, acc_ref, sem = rest[-4:]
    carry_on(sz, plan_ref, before_ref, acc_ref)
    run_stage(sz, 1, plan_ref, sources, a_ref, None, b_ref, acc_ref)

    def store(n):
        target = plan_ref[sz.targets_at + n]
        pltpu.make_async_copy(place(acc_ref, target), block_at(out_ref, target // sz.cols, target % sz.cols), sem).start()

    n_targets = plan_ref[sz.counts_at + 2 * sz.stages]
    repeat(0, n_targets, store)
    repeat(0, n_targets, lambda n: pltpu.make_async_copy(place(acc_ref, 0), block_at(out_ref, 0, 0), sem).wait())


def swaps(size, m):
    return [(i, i ^ m) for i in range(size)]


def exchange_and_multiply(sz, lengths, matrix, table, near_list):
    n_x = sz.n_row - 1
    far_length, side_length, row_length, near_length = lengths
    smem = pl.BlockSpec(memory_space=pltpu.SMEM)
    vmem = pl.BlockSpec(memory_space=pltpu.VMEM)
    anywhere = pl.BlockSpec(memory_space=pltpu.HBM)
    params = pltpu.CompilerParams(vmem_limit_bytes=(24 if far_length < sz.cap else 44) * 2**20)
    small = pl.CostEstimate(flops=0, bytes_accessed=1024, transcendentals=0)

    def blocks(n):
        return jax.ShapeDtypeStruct((n * BS + 8, BS), jnp.float32)

    shapes = [jax.ShapeDtypeStruct((sz.own * BS, BS), jnp.float32), blocks(near_length), blocks(side_length)]
    shapes += [blocks(far_length)] * (sz.n_col - 2) + [blocks(row_length)] * n_x
    own, near, *lists = pl.pallas_call(
        functools.partial(pack_kernel, sz),
        out_shape=shapes,
        in_specs=[smem, smem, anywhere],
        out_specs=[vmem] * len(shapes),
        scratch_shapes=[pltpu.SemaphoreType.DMA((sz.own,))],
        compiler_params=params,
        cost_estimate=small,
        name="pack",
    )(table, near_list, matrix)
    zs = [lax.ppermute(x, "col", swaps(sz.n_col, m + 1)) for m, x in enumerate(lists[: sz.n_col - 1])]
    xs = [lax.ppermute(x, "row", swaps(sz.n_row, m + 1)) for m, x in enumerate(lists[sz.n_col - 1 :])]
    plan, zeros = pl.pallas_call(
        functools.partial(plan_kernel, sz),
        out_shape=[jax.ShapeDtypeStruct((sz.n_plan,), jnp.int32), jax.ShapeDtypeStruct(matrix.shape, matrix.dtype)],
        in_specs=[smem, smem],
        out_specs=[smem, anywhere],
        scratch_shapes=[
            pltpu.SMEM((sz.n_load,), jnp.int32),
            pltpu.SMEM((sz.n_out,), jnp.int32),
            pltpu.VMEM((BS, matrix.shape[1]), jnp.float32),
            pltpu.SemaphoreType.DMA,
        ],
        cost_estimate=small,
        name="plan",
    )(table, near_list)
    zs[0], plan = lax.optimization_barrier((zs[0], plan))

    def across(q, x):
        return lax.ppermute(x, "depth", swaps(sz.n_depth, q))

    numbers, sources = list(range(2 + n_x)), [own, *xs, zs[0]]
    a_shape = ((sz.n_a * BS, 3 * BS), jnp.bfloat16)
    acc_shape = (((sz.n_out + 1) * BS, BS), jnp.float32)
    right, acc = pl.pallas_call(
        functools.partial(early_kernel, sz, numbers),
        out_shape=[
            jax.ShapeDtypeStruct((3 * sz.own * BS, BS), jnp.bfloat16),
            jax.ShapeDtypeStruct(*acc_shape),
        ],
        in_specs=[smem] + [vmem] * len(sources),
        out_specs=[vmem] * 2,
        scratch_shapes=[pltpu.VMEM(*a_shape)],
        compiler_params=params,
        cost_estimate=small,
        name="early",
    )(plan, *sources)
    *far, acc = lax.optimization_barrier((*zs[1:], acc))
    numbers, sources = [2 + n_x + m for m in range(len(far))], list(far)
    for q in range(1, sz.n_depth):
        base = 1 + n_x + q * sz.block
        numbers += [base - 1, base] + [base + 1 + m for m in range(len(far))]
        sources += [across(q, x) for x in (near, zs[0], *far)]
    return pl.pallas_call(
        functools.partial(late_kernel, sz, numbers),
        out_shape=jax.ShapeDtypeStruct(matrix.shape, matrix.dtype),
        in_specs=[smem, anywhere] + [vmem] * (2 + len(sources)),
        out_specs=anywhere,
        input_output_aliases={1: 0},
        scratch_shapes=[pltpu.VMEM(*a_shape), pltpu.VMEM(*acc_shape), pltpu.SemaphoreType.DMA],
        compiler_params=params,
        cost_estimate=small,
        name="late",
    )(plan, zeros, right, acc, *sources)


def shards(sz, matrix, occupancy, pattern):
    smem = pl.BlockSpec(memory_space=pltpu.SMEM)
    vmem = pl.BlockSpec(memory_space=pltpu.VMEM)
    table, near_list, bucket = pl.pallas_call(
        functools.partial(table_kernel, sz),
        out_shape=[
            jax.ShapeDtypeStruct((sz.tables, sz.nb, sz.nb), jnp.int32),
            jax.ShapeDtypeStruct((1, sz.nb), jnp.int32),
            jax.ShapeDtypeStruct((1,), jnp.int32),
        ],
        in_specs=[vmem, vmem],
        out_specs=[vmem, vmem, smem],
        name="tables",
    )(occupancy, pattern)
    branches = [functools.partial(exchange_and_multiply, sz, lengths) for lengths in sz.lengths]
    return lax.switch(bucket[0], branches, matrix, table, near_list)


def solution(mesh):
    def whole(matrix, occupancy, pattern):
        sz = Sizes(mesh, matrix.shape)
        return jax.shard_map(
            functools.partial(shards, sz),
            mesh=mesh,
            in_specs=(P("row", ("col", "depth")), P(), P()),
            out_specs=P("row", ("col", "depth")),
            check_vma=False,
        )(matrix, occupancy, pattern)

    return whole
```
